32 devices in a mesh: ray: 8 (over z, y), pix: 4 (over x, core).
Axes of the slice: x: 2, y: 2, z: 4, core: 2. Of those that a mesh axis runs over, the one named last changes fastest.
Arguments:
- positions: float32 [2, 8192], P(None, 'ray'), may hold values from -2 to 2
- directions: float32 [2, 8192], P(None, 'ray'), may hold values from -0.35 to 0.35
- path: float32 [8192], P('ray'), may hold values from -9 to 9
- amplitude: float32 [8192], P('ray'), may hold values from 0.3 to 3
- psf_grad: float32 [3, 1024, 1024], P(None, 'pix', 'ray'), may hold values from -0.3 to 0.3
Outputs:
- psf: float32 [3, 1024, 1024], P(None, 'pix', 'ray')
- ray_grad: float32 [6, 8192], P(None, 'ray')
The draws below stay inside these ranges and needn't reach their ends.
All inputs are finite; a program needn't handle non-finite values.
Results may differ from the reference program's by a relative error of at most 0.0054.
Values may be sent and summed in bfloat16 or wider, within the bound.
No kernel may reach another device: no remote copies, remote signals or barrier semaphores. Data moves between devices by JAX's collectives and lax.ppermute only.
A program may use at most 192 MiB of HBM per device.

```python
import math
import jax
import jax.numpy as jnp
from jax import lax

NPIX = 1024
NRAY = 8192


def levels(stream_key, shape, pieces, smallest, high):
    def one(dim, blocks):
        steps = jax.random.uniform(jax.random.fold_in(jax.random.fold_in(stream_key, 6), dim), (blocks,), jnp.float32, smallest / len(pieces), high / len(pieces))
        return jnp.repeat(jnp.exp(steps), shape[dim] // blocks).reshape((-1,) + (1,) * (len(shape) - dim - 1))

    loudness = one(*pieces[0])
    for cut in pieces[1:]:
        loudness = loudness * one(*cut)
    return loudness


def normal_values(key, extent, width, most, shards=(), kind=jnp.bfloat16):
    factor_of = levels(key, extent, shards, -0.22, 0.18) if shards else 1.0
    array = jax.random.normal(key, extent, jnp.float32) * width * factor_of
    return jnp.minimum(jnp.maximum(array, -most), most).astype(kind)


def setup_inputs(seed: int = 0) -> dict:
    key_of = jax.random.split(jax.random.key(seed), 6)
    positions = jnp.clip(jax.random.uniform(key_of[0], (2, NRAY), jnp.float32, -2.0, 2.0) * levels(key_of[0], (2, NRAY), ((1, 8),), -0.4, 0.0), -2.0, 2.0)
    directions = jnp.clip(jax.random.uniform(key_of[1], (2, NRAY), jnp.float32, -0.35, 0.35) * levels(key_of[1], (2, NRAY), ((1, 8),), -0.4, 0.0), -0.35, 0.35)
    path = normal_values(key_of[2], (NRAY,), 3.0, 9.0, ((0, 8),), jnp.float32)
    amplitude = jnp.clip(jnp.exp(math.log(3.0) - 2.3025851 * jax.random.uniform(key_of[3], (NRAY,), jnp.float32) ** levels(key_of[3], (NRAY,), ((0, 8),), -0.2, 0.2)), 0.3, 3.0)
    psf_grad = normal_values(key_of[4], (3, NPIX, NPIX), 0.05, 0.3, ((1, 4), (2, 8)), jnp.float32)
    return {"positions": positions, "directions": directions, "path": path, "amplitude": amplitude, "psf_grad": psf_grad}


wave_scales = (1.2088, 1.0, 0.8953)
two_pi = 2.0 * math.pi
highest = lax.Precision.HIGHEST

def centred(start, count):
    return (start + jnp.arange(count)).astype(jnp.float32) - 0.5 * NPIX + 0.5

def row_tables(block, rows_x, scale, norm):
    angle = scale * (block[4][:, None] + two_pi * (block[2][:, None] * (rows_x[None, :] - block[0][:, None]) - block[3][:, None] * block[1][:, None]))
    weight = (block[5] * norm)[:, None]
    return (weight * jnp.cos(angle), weight * jnp.sin(angle))

def col_tables(block, cols_y, scale):
    angle = scale * two_pi * cols_y[:, None] * block[3][None, :]
    return (jnp.cos(angle), jnp.sin(angle))

def mixing(a_re, a_im):
    upper = jnp.concatenate([a_re, a_im], axis=1)
    lower = jnp.concatenate([-a_im, a_re], axis=1)
    return jnp.concatenate([upper, lower], axis=0).astype(jnp.bfloat16)

def product(left, right, dims):
    return lax.dot_general(left.astype(jnp.float32), right.astype(jnp.float32), dims, precision=highest, preferred_element_type=jnp.float32)

def block_count(count):
    return max(1, min(16, count // 256))

def field_terms(rays, rows_x, cols_y, norm):
    count = rays.shape[1]
    nblk = block_count(count)
    blk = count // nblk

    def step(index, total):
        block = lax.dynamic_slice_in_dim(rays, (index * blk).astype(jnp.int32), blk, 1)
        parts = []
        for wave in range(3):
            scale = wave_scales[wave]
            a_re, a_im = row_tables(block, rows_x, scale, norm)
            b_re, b_im = col_tables(block, cols_y, scale)
            left = jnp.concatenate([b_re, b_im], axis=1).astype(jnp.bfloat16)
            parts.append(product(left, mixing(a_re, a_im), (((1,), (0,)), ((), ()))))
        return total + jnp.concatenate(parts, axis=1)
    init = jnp.zeros((cols_y.shape[0], 6 * rows_x.shape[0]), jnp.float32)
    return lax.fori_loop(0, nblk, step, init)

def ray_partials(rays, rows_x, cols_y, cotangent, norm):
    count = rays.shape[1]
    nblk = block_count(count)
    blk = count // nblk
    plen = rows_x.shape[0]

    def one_block(index):
        block = lax.dynamic_slice_in_dim(rays, (index * blk).astype(jnp.int32), blk, 1)
        first = jnp.zeros((blk,), jnp.float32)
        second = jnp.zeros((blk,), jnp.float32)
        third = jnp.zeros((blk,), jnp.float32)
        fourth = jnp.zeros((blk,), jnp.float32)
        for wave in range(3):
            scale = wave_scales[wave]
            a_re, a_im = row_tables(block, rows_x, scale, norm)
            b_re, b_im = col_tables(block, cols_y, scale)
            left = jnp.concatenate([b_re, b_im], axis=1).astype(jnp.bfloat16)
            mix = mixing(a_re, a_im)
            grad_u = cotangent[:, 2 * plen * wave:2 * plen * (wave + 1)]
            proj = product(left, grad_u, (((0,), (0,)), ((), ())))
            d_are = proj[:blk, :plen] + proj[blk:, plen:]
            d_aim = proj[:blk, plen:] - proj[blk:, :plen]
            d_b = product(grad_u, mix, (((1,), (1,)), ((), ())))
            d_beta = d_b[:, blk:] * b_re - d_b[:, :blk] * b_im
            d_alpha = d_aim * a_re - d_are * a_im
            first = first + scale * lax.optimization_barrier(jnp.sum(d_alpha, axis=1))
            second = second + scale * two_pi * lax.optimization_barrier(jnp.sum(d_alpha * rows_x[None, :], axis=1))
            third = third + scale * two_pi * lax.optimization_barrier(jnp.sum(d_beta * cols_y[:, None], axis=0))
            fourth = fourth + lax.optimization_barrier(jnp.sum(d_are * a_re + d_aim * a_im, axis=1))
        return jnp.stack([first, second, third, fourth])
    out = lax.map(one_block, jnp.arange(nblk))
    return jnp.transpose(out, (1, 0, 2)).reshape(4, count)

def finish(sums, rays):
    return jnp.stack([sums[0], -two_pi * rays[2] * sums[0], -two_pi * rays[3] * sums[0], (sums[1] - two_pi * rays[0] * sums[0]) / NPIX, (sums[2] - two_pi * rays[1] * sums[0]) / NPIX, sums[3] / rays[5]])

def reference(positions, directions, path, amplitude, psf_grad):
    rays = jnp.concatenate([positions, directions, path[None], amplitude[None]], axis=0)
    coords = centred(0, NPIX)
    norm = 1.0 / math.sqrt(NRAY)
    field = field_terms(rays, coords, coords, norm).reshape(NPIX, 3, 2, NPIX)
    psf = jnp.transpose(field[:, :, 0] ** 2 + field[:, :, 1] ** 2, (1, 2, 0))
    weight = jnp.transpose(psf_grad, (2, 0, 1))
    grad_u = (2.0 * weight[:, :, None, :] * field).reshape(NPIX, 6 * NPIX).astype(jnp.bfloat16)
    sums = ray_partials(rays, coords, coords, grad_u, norm)
    return (psf, finish(sums, rays))
```

```python
import functools
import math

import jax
import jax.numpy as jnp
from jax import lax
from jax.experimental import pallas as pl
from jax.experimental.pallas import tpu as pltpu
from jax.sharding import PartitionSpec as P

NPIX = 1024
LANES = 128
CHUNK = 256
TILES = CHUNK // LANES

wave_scales = (1.2088, 1.0, 0.8953)
two_pi = 2.0 * math.pi
sin_terms = [(-1.0) ** n / math.factorial(2 * n + 1) * (0.5 * math.pi) ** (2 * n + 1) for n in range(5)]
cos_terms = [(-1.0) ** n / math.factorial(2 * n) * (0.5 * math.pi) ** (2 * n) for n in range(6)]


def horner(square, terms):
    value = terms[-1]
    for term in terms[-2::-1]:
        value = value * square + term
    return value


def circle(turns):
    rest = turns - jnp.floor(turns + 0.5)
    square = rest * rest
    sin = rest * horner(square, sin_terms)
    cos = horner(square, cos_terms)
    sin, cos = 2.0 * sin * cos, 1.0 - 2.0 * sin * sin
    return 1.0 - 2.0 * sin * sin, 2.0 * sin * cos


def times(left, right):
    return (left[0] * right[0] - left[1] * right[1], left[0] * right[1] + left[1] * right[0])


def ladder(first, second, twice, count):
    out = [first, second]
    while len(out) < count:
        out.append(twice * out[-1] - out[-2])
    return out[:count]


def psf_kernel(sizes, own_ref, near_ref, far_ref, extra_ref, grad_ref, psf_ref, own_out, near_out, far_out, extra_out,
               rays_s, row_base, col_base, steps, row_tab, col_tab, col_half, field, cot, sums):
    shards, local, plen, clen, half, pairs, norm = sizes
    x_mid = (lax.axis_index("pix") * plen).astype(jnp.float32) + (0.5 * plen - 0.5 * NPIX)
    y_low = (lax.axis_index("ray") * clen).astype(jnp.float32) + (0.5 - 0.5 * NPIX)

    split = local // CHUNK

    def place(slot, block):
        for item in range(6):
            rays_s[item, slot : slot + 1, :] = block[item : item + 1, :]

    place(0, own_ref[...])
    for index in range(pairs):
        place(1 + index, near_ref[index])
        place(1 + pairs + index, far_ref[index])
    place(1 + 2 * pairs, extra_ref[...])

    def spread(base, wave, part, sub, piece, value):
        for tile in range(TILES):
            base[wave, part, piece * TILES + tile, pl.ds(sub, shards, stride=8), :] = value[:, tile * LANES : (tile + 1) * LANES]

    def gather(base, wave, part, shard, chunk):
        rows8 = pl.ds(pl.multiple_of(shard * 8, 8), 8)
        first = lax.rem(chunk, split) * TILES
        return jnp.concatenate([base[wave, part, first + tile, rows8, :] for tile in range(TILES)], axis=1)

    @pl.loop(0, local // CHUNK)
    def _(piece):
        lanes = pl.ds(pl.multiple_of(piece * CHUNK, CHUNK), CHUNK)
        x, y, dir_l, dir_m, path, amp = [rays_s[item, :, lanes] for item in range(6)]
        phase = path * (1.0 / two_pi) + (dir_l * (x_mid - x) + dir_m * (y_low - y))
        amp = amp * norm
        for wave in range(3):
            scale = wave_scales[wave]
            value = circle((0.5 * scale) * dir_l)
            one = times(value, value)
            for sub in range(8):
                spread(row_base, wave, 0, sub, piece, value[0])
                spread(row_base, wave, 1, sub, piece, value[1])
                value = times(value, one)
            two = times(one, one)
            four = times(two, two)
            eight = times(four, four)
            steps[wave, 0, :, lanes] = eight[0]
            steps[wave, 1, :, lanes] = eight[1]
            cos, sin = circle(scale * phase)
            value = (amp * cos, amp * sin)
            one = circle(scale * dir_m)
            for sub in range(8):
                spread(col_base, wave, 0, sub, piece, value[0])
                spread(col_base, wave, 1, sub, piece, value[1])
                value = times(value, one)
            two = times(one, one)
            four = times(two, two)
            eight = times(four, four)
            steps[wave, 2, :, lanes] = eight[0]
            steps[wave, 3, :, lanes] = eight[1]

    field[...] = jnp.zeros_like(field)

    def where(chunk):
        return chunk // split, pl.ds(pl.multiple_of(lax.rem(chunk, split) * CHUNK, CHUNK), CHUNK)

    @pl.loop(0, shards * split)
    def _(chunk):
        shard, lanes = where(chunk)
        for wave in range(3):
            for base, step, tall, is_row in ((row_base, 0, half, True), (col_base, 2, clen, False)):
                c8 = jnp.broadcast_to(steps[wave, step, pl.ds(shard, 1), lanes], (8, CHUNK))
                s8 = jnp.broadcast_to(steps[wave, step + 1, pl.ds(shard, 1), lanes], (8, CHUNK))
                first = (gather(base, wave, 0, shard, chunk), gather(base, wave, 1, shard, chunk))
                second = times(first, (c8, s8))
                twice = 2.0 * c8
                for part in range(2):
                    run = ladder(first[part], second[part], twice, tall // 8)
                    for pair in range(tall // 16):
                        both = jnp.concatenate(run[2 * pair : 2 * pair + 2], axis=0)
                        place16 = pl.ds(part * tall + 16 * pair, 16)
                        if is_row:
                            row_tab[wave, chunk, place16, :] = both.astype(jnp.bfloat16)
                        else:
                            col_tab[wave, chunk, place16, :] = both
                            col_half[wave, place16, :] = both.astype(jnp.bfloat16)
            field[wave] += lax.dot_general(
                col_half[wave], row_tab[wave, chunk], (((1,), (1,)), ((), ())), preferred_element_type=jnp.float32
            )

    offset = lax.broadcasted_iota(jnp.int32, (8, half), 1).astype(jnp.float32) + 0.5
    for wave in range(3):
        for group in range(clen // 8):
            rows = slice(8 * group, 8 * group + 8)
            low = slice(clen + 8 * group, clen + 8 * group + 8)
            even_r, odd_r = field[wave, rows, :half], field[wave, rows, half:]
            even_i, odd_i = field[wave, low, :half], field[wave, low, half:]
            up_r, up_i = even_r - odd_i, even_i + odd_r
            dn_r, dn_i = even_r + odd_i, even_i - odd_r
            psf_ref[wave, 0, rows, :] = dn_r * dn_r + dn_i * dn_i
            psf_ref[wave, 1, rows, :] = up_r * up_r + up_i * up_i
            g_dn = 2.0 * grad_ref[wave, 0, rows, :]
            g_up = 2.0 * grad_ref[wave, 1, rows, :]
            dn_r, dn_i, up_r, up_i = g_dn * dn_r, g_dn * dn_i, g_up * up_r, g_up * up_i
            p_r, p_i, m_r, m_i = up_r + dn_r, up_i + dn_i, up_r - dn_r, up_i - dn_i
            plain = jnp.concatenate(
                [jnp.concatenate([p_r, m_i], axis=1), jnp.concatenate([p_i, -m_r], axis=1)], axis=0
            )
            heavy = jnp.concatenate(
                [
                    jnp.concatenate([offset * m_r, offset * p_i], axis=1),
                    jnp.concatenate([offset * m_i, -(offset * p_r)], axis=1),
                ],
                axis=0,
            )
            cot[wave, 32 * group : 32 * group + 16, :] = plain.astype(jnp.bfloat16)
            cot[wave, 32 * group + 16 : 32 * group + 32, :] = heavy.astype(jnp.bfloat16)

    sub = lax.broadcasted_iota(jnp.int32, (8, CHUNK), 0).astype(jnp.float32)
    y_sub = sub + (y_low + clen)

    @pl.loop(0, shards * split)
    def _(chunk):
        shard, lanes = where(chunk)
        total = [jnp.zeros((8, CHUNK), jnp.float32) for _ in range(4)]
        for wave in range(3):
            scale = wave_scales[wave]
            back = jnp.dot(cot[wave], row_tab[wave, chunk], preferred_element_type=jnp.float32)
            im_sum = jnp.zeros((8, CHUNK), jnp.float32)
            up_sum = jnp.zeros((8, CHUNK), jnp.float32)
            re_sum = jnp.zeros((8, CHUNK), jnp.float32)
            x_sum = jnp.zeros((8, CHUNK), jnp.float32)
            for group in range(clen // 8):
                e_r, e_i, f_r, f_i = [back[32 * group + 8 * n : 32 * group + 8 * n + 8] for n in range(4)]
                b_r = col_tab[wave, chunk, 8 * group : 8 * group + 8, :]
                b_i = col_tab[wave, chunk, clen + 8 * group : clen + 8 * group + 8, :]
                im_sum = im_sum + (b_r * e_i - b_i * e_r)
                re_sum = re_sum + (b_r * e_r + b_i * e_i)
                x_sum = x_sum + (b_r * f_i - b_i * f_r)
                up_sum = up_sum + im_sum
            total[0] = total[0] + scale * im_sum
            total[1] = total[1] + (scale * two_pi) * (x_mid * im_sum + x_sum)
            total[2] = total[2] + (scale * two_pi) * (y_sub * im_sum - 8.0 * up_sum)
            total[3] = total[3] + re_sum
        rows = [jnp.sum(value, axis=0, keepdims=True) for value in total]
        sums[shard, :, lanes] = jnp.concatenate(rows, axis=0)

    own_out[...] = sums[0]
    for index in range(pairs):
        near_out[index] = sums[1 + index]
        far_out[index] = sums[1 + pairs + index]
    extra_out[...] = sums[1 + 2 * pairs]


def split_pairs(shards):
    if shards == 8:
        return ((3, 7), (1, 6), (2, 4)), 5
    pairs = (shards - 2) // 2
    return tuple((1 + n, 1 + pairs + n) for n in range(pairs)), shards - 1


def on_device(positions, directions, path, amplitude, psf_grad):
    rays = jnp.concatenate([positions, directions, path[None], amplitude[None]], axis=0)
    local = rays.shape[1]
    shards = lax.axis_size("ray")
    rows = lax.axis_size("pix")
    plen = NPIX // rows
    clen = NPIX // shards
    half = max(plen // 2, LANES)
    norm = 1.0 / math.sqrt(local * shards)
    pairs, last = split_pairs(shards)
    count = len(pairs)

    def swap(value, ray_even, ray_odd, pix=0):
        moves = []
        for r in range(shards):
            for p in range(rows):
                moves.append((r * rows + p, (r ^ (ray_odd if p % 2 else ray_even)) * rows + (p ^ pix)))
        return lax.ppermute(value, ("ray", "pix"), moves)

    near = jnp.stack([swap(rays, even, odd) for even, odd in pairs])
    extra = swap(rays, last, last)
    far = swap(near, 0, 0, 1)

    weight = psf_grad.reshape(3, 2, plen // 2, clen)
    weight = jnp.stack([weight[:, 0, ::-1], weight[:, 1]], axis=1).transpose(0, 1, 3, 2)
    if half != plen // 2:
        weight = jnp.pad(weight, ((0, 0), (0, 0), (0, 0), (0, half - plen // 2)))

    chunks = shards * (local // CHUNK)
    sizes = (shards, local, plen, clen, half, count, norm)
    f32, bf16 = jnp.float32, jnp.bfloat16
    vmem = pl.BlockSpec(memory_space=pltpu.VMEM)
    psf, own_sum, near_sum, far_sum, extra_sum = pl.pallas_call(
        functools.partial(psf_kernel, sizes),
        out_shape=[
            jax.ShapeDtypeStruct((3, 2, clen, half), f32),
            jax.ShapeDtypeStruct((4, local), f32),
            jax.ShapeDtypeStruct((count, 4, local), f32),
            jax.ShapeDtypeStruct((count, 4, local), f32),
            jax.ShapeDtypeStruct((4, local), f32),
        ],
        in_specs=[vmem] * 5,
        out_specs=[vmem] * 5,
        scratch_shapes=[
            pltpu.VMEM((6, shards, local), f32),
            pltpu.VMEM((3, 2, local // LANES, 8 * shards, LANES), f32),
            pltpu.VMEM((3, 2, local // LANES, 8 * shards, LANES), f32),
            pltpu.VMEM((3, 4, shards, local), f32),
            pltpu.VMEM((3, chunks, 2 * half, CHUNK), bf16),
            pltpu.VMEM((3, chunks, 2 * clen, CHUNK), f32),
            pltpu.VMEM((3, 2 * clen, CHUNK), bf16),
            pltpu.VMEM((3, 2 * clen, 2 * half), f32),
            pltpu.VMEM((3, 4 * clen, 2 * half), bf16),
            pltpu.VMEM((shards, 4, local), f32),
        ],
        compiler_params=pltpu.CompilerParams(vmem_limit_bytes=62 * 1024 * 1024),
    )(rays, near, far, extra, weight)

    psf = psf[..., : plen // 2].transpose(0, 1, 3, 2)
    psf = jnp.concatenate([psf[:, 0, ::-1], psf[:, 1]], axis=1)

    near_sum = near_sum + swap(far_sum, 0, 0, 1)
    total = own_sum + swap(extra_sum, last, last)
    for index, (even, odd) in enumerate(pairs):
        total = total + swap(near_sum[index], even, odd)
    bit = 1
    parts = total
    while bit < rows:
        parts = parts + swap(parts, 0, 0, bit)
        bit *= 2
    sums = parts
    grads = jnp.stack(
        [
            sums[0],
            -two_pi * rays[2] * sums[0],
            -two_pi * rays[3] * sums[0],
            (sums[1] - two_pi * rays[0] * sums[0]) / NPIX,
            (sums[2] - two_pi * rays[1] * sums[0]) / NPIX,
            sums[3] / rays[5],
        ]
    )
    return (psf, grads)


def solution(mesh):
    in_specs = (P(None, "ray"), P(None, "ray"), P("ray"), P("ray"), P(None, "pix", "ray"))
    out_specs = (P(None, "pix", "ray"), P(None, "ray"))
    return jax.shard_map(on_device, mesh=mesh, in_specs=in_specs, out_specs=out_specs, check_vma=False)
```

```python
import functools
import math

import jax
import jax.numpy as jnp
from jax import lax
from jax.experimental import pallas as pl
from jax.experimental.pallas import tpu as pltpu
from jax.sharding import PartitionSpec as P

NPIX = 1024
LANES = 128
CHUNK = 1024
TILES = CHUNK // LANES

wave_scales = (1.2088, 1.0, 0.8953)
two_pi = 2.0 * math.pi
sin_terms = [(-1.0) ** n / math.factorial(2 * n + 1) * (0.5 * math.pi) ** (2 * n + 1) for n in range(5)]
cos_terms = [(-1.0) ** n / math.factorial(2 * n) * (0.5 * math.pi) ** (2 * n) for n in range(6)]


def horner(square, terms):
    value = terms[-1]
    for term in terms[-2::-1]:
        value = value * square + term
    return value


def circle(turns):
    rest = turns - jnp.floor(turns + 0.5)
    square = rest * rest
    sin = rest * horner(square, sin_terms)
    cos = horner(square, cos_terms)
    sin, cos = 2.0 * sin * cos, 1.0 - 2.0 * sin * sin
    return 1.0 - 2.0 * sin * sin, 2.0 * sin * cos


def times(left, right):
    return (left[0] * right[0] - left[1] * right[1], left[0] * right[1] + left[1] * right[0])


def ladder(first, second, twice, count):
    out = [first, second]
    while len(out) < count:
        out.append(twice * out[-1] - out[-2])
    return out[:count]


def psf_kernel(sizes, own_ref, near_ref, far_ref, extra_ref, grad_ref, psf_ref, own_out, near_out, far_out, extra_out,
               rays_s, row_base, col_base, steps, sums, *tables):
    shards, local, plen, clen, half, pairs, norm = sizes
    row_tab, col_tab, col_half, field, cot = [tables[3 * n : 3 * n + 3] for n in range(5)]
    x_mid = (lax.axis_index("pix") * plen).astype(jnp.float32) + (0.5 * plen - 0.5 * NPIX)
    y_low = (lax.axis_index("ray") * clen).astype(jnp.float32) + (0.5 - 0.5 * NPIX)

    split = local // CHUNK

    def place(slot, block):
        for item in range(6):
            rays_s[item, slot : slot + 1, :] = block[item : item + 1, :]

    place(0, own_ref[...])
    for index in range(pairs):
        place(1 + index, near_ref[index])
        place(1 + pairs + index, far_ref[index])
    place(1 + 2 * pairs, extra_ref[...])

    def spread(base, wave, part, sub, piece, value):
        for tile in range(TILES):
            base[wave, part, piece * TILES + tile, pl.ds(sub, shards, stride=8), :] = value[:, tile * LANES : (tile + 1) * LANES]

    def gather(base, wave, part, shard, chunk):
        rows8 = pl.ds(pl.multiple_of(shard * 8, 8), 8)
        first = lax.rem(chunk, split) * TILES
        return jnp.concatenate([base[wave, part, first + tile, rows8, :] for tile in range(TILES)], axis=1)

    @pl.loop(0, local // CHUNK)
    def _(piece):
        lanes = pl.ds(pl.multiple_of(piece * CHUNK, CHUNK), CHUNK)
        x, y, dir_l, dir_m, path, amp = [rays_s[item, :, lanes] for item in range(6)]
        phase = path * (1.0 / two_pi) + (dir_l * (x_mid - x) + dir_m * (y_low - y))
        amp = amp * norm
        for wave in range(3):
            scale = wave_scales[wave]
            value = circle((0.5 * scale) * dir_l)
            one = times(value, value)
            for sub in range(8):
                spread(row_base, wave, 0, sub, piece, value[0])
                spread(row_base, wave, 1, sub, piece, value[1])
                value = times(value, one)
            two = times(one, one)
            four = times(two, two)
            eight = times(four, four)
            steps[wave, 0, :, lanes] = eight[0]
            steps[wave, 1, :, lanes] = eight[1]
            cos, sin = circle(scale * phase)
            value = (amp * cos, amp * sin)
            one = circle(scale * dir_m)
            for sub in range(8):
                spread(col_base, wave, 0, sub, piece, value[0])
                spread(col_base, wave, 1, sub, piece, value[1])
                value = times(value, one)
            two = times(one, one)
            four = times(two, two)
            eight = times(four, four)
            steps[wave, 2, :, lanes] = eight[0]
            steps[wave, 3, :, lanes] = eight[1]

    for wave in range(3):
        field[wave][...] = jnp.zeros_like(field[wave])

    def where(chunk):
        return chunk // split, pl.ds(pl.multiple_of(lax.rem(chunk, split) * CHUNK, CHUNK), CHUNK)

    @pl.loop(0, shards * split)
    def _(chunk):
        shard, lanes = where(chunk)
        for wave in range(3):
            for base, step, tall, is_row in ((row_base, 0, half, True), (col_base, 2, clen, False)):
                c8 = jnp.broadcast_to(steps[wave, step, pl.ds(shard, 1), lanes], (8, CHUNK))
                s8 = jnp.broadcast_to(steps[wave, step + 1, pl.ds(shard, 1), lanes], (8, CHUNK))
                first = (gather(base, wave, 0, shard, chunk), gather(base, wave, 1, shard, chunk))
                second = times(first, (c8, s8))
                twice = 2.0 * c8
                for part in range(2):
                    run = ladder(first[part], second[part], twice, tall // 8)
                    for pair in range(tall // 16):
                        both = jnp.concatenate(run[2 * pair : 2 * pair + 2], axis=0)
                        place16 = pl.ds(part * tall + 16 * pair, 16)
                        if is_row:
                            row_tab[wave][chunk, place16, :] = both.astype(jnp.bfloat16)
                        else:
                            col_tab[wave][chunk, place16, :] = both
                            col_half[wave][place16, :] = both.astype(jnp.bfloat16)
            field[wave][...] += lax.dot_general(
                col_half[wave][...], row_tab[wave][chunk], (((1,), (1,)), ((), ())), preferred_element_type=jnp.float32
            )

    offset = lax.broadcasted_iota(jnp.int32, (8, half), 1).astype(jnp.float32) + 0.5
    for wave in range(3):
        for group in range(clen // 8):
            rows = slice(8 * group, 8 * group + 8)
            low = slice(clen + 8 * group, clen + 8 * group + 8)
            even_r, odd_r = field[wave][rows, :half], field[wave][rows, half:]
            even_i, odd_i = field[wave][low, :half], field[wave][low, half:]
            up_r, up_i = even_r - odd_i, even_i + odd_r
            dn_r, dn_i = even_r + odd_i, even_i - odd_r
            psf_ref[wave, 0, rows, :] = dn_r * dn_r + dn_i * dn_i
            psf_ref[wave, 1, rows, :] = up_r * up_r + up_i * up_i
            g_dn = 2.0 * grad_ref[wave, 0, rows, :]
            g_up = 2.0 * grad_ref[wave, 1, rows, :]
            dn_r, dn_i, up_r, up_i = g_dn * dn_r, g_dn * dn_i, g_up * up_r, g_up * up_i
            p_r, p_i, m_r, m_i = up_r + dn_r, up_i + dn_i, up_r - dn_r, up_i - dn_i
            plain = jnp.concatenate(
                [jnp.concatenate([p_r, m_i], axis=1), jnp.concatenate([p_i, -m_r], axis=1)], axis=0
            )
            heavy = jnp.concatenate(
                [
                    jnp.concatenate([offset * m_r, offset * p_i], axis=1),
                    jnp.concatenate([offset * m_i, -(offset * p_r)], axis=1),
                ],
                axis=0,
            )
            cot[wave][32 * group : 32 * group + 16, :] = plain.astype(jnp.bfloat16)
            cot[wave][32 * group + 16 : 32 * group + 32, :] = heavy.astype(jnp.bfloat16)

    sub = lax.broadcasted_iota(jnp.int32, (8, CHUNK), 0).astype(jnp.float32)
    y_sub = sub + (y_low + clen)

    @pl.loop(0, shards * split)
    def _(chunk):
        shard, lanes = where(chunk)
        total = [jnp.zeros((8, CHUNK), jnp.float32) for _ in range(4)]
        for wave in range(3):
            scale = wave_scales[wave]
            back = jnp.dot(cot[wave][...], row_tab[wave][chunk], preferred_element_type=jnp.float32)
            im_sum = jnp.zeros((8, CHUNK), jnp.float32)
            up_sum = jnp.zeros((8, CHUNK), jnp.float32)
            re_sum = jnp.zeros((8, CHUNK), jnp.float32)
            x_sum = jnp.zeros((8, CHUNK), jnp.float32)
            for group in range(clen // 8):
                e_r, e_i, f_r, f_i = [back[32 * group + 8 * n : 32 * group + 8 * n + 8] for n in range(4)]
                b_r = col_tab[wave][chunk, 8 * group : 8 * group + 8, :]
                b_i = col_tab[wave][chunk, clen + 8 * group : clen + 8 * group + 8, :]
                im_sum = im_sum + (b_r * e_i - b_i * e_r)
                re_sum = re_sum + (b_r * e_r + b_i * e_i)
                x_sum = x_sum + (b_r * f_i - b_i * f_r)
                up_sum = up_sum + im_sum
            total[0] = total[0] + scale * im_sum
            total[1] = total[1] + (scale * two_pi) * (x_mid * im_sum + x_sum)
            total[2] = total[2] + (scale * two_pi) * (y_sub * im_sum - 8.0 * up_sum)
            total[3] = total[3] + re_sum
        rows = [jnp.sum(value, axis=0, keepdims=True) for value in total]
        sums[shard, :, lanes] = jnp.concatenate(rows, axis=0)

    own_out[...] = sums[0]
    for index in range(pairs):
        near_out[index] = sums[1 + index]
        far_out[index] = sums[1 + pairs + index]
    extra_out[...] = sums[1 + 2 * pairs]


def split_pairs(shards):
    if shards == 8:
        return ((3, 7), (1, 6), (2, 4)), 5
    pairs = (shards - 2) // 2
    return tuple((1 + n, 1 + pairs + n) for n in range(pairs)), shards - 1


def on_device(positions, directions, path, amplitude, psf_grad):
    rays = jnp.concatenate([positions, directions, path[None], amplitude[None]], axis=0)
    local = rays.shape[1]
    shards = lax.axis_size("ray")
    rows = lax.axis_size("pix")
    plen = NPIX // rows
    clen = NPIX // shards
    half = max(plen // 2, LANES)
    norm = 1.0 / math.sqrt(local * shards)
    pairs, last = split_pairs(shards)
    count = len(pairs)

    def swap(value, ray_even, ray_odd, pix=0):
        moves = []
        for r in range(shards):
            for p in range(rows):
                moves.append((r * rows + p, (r ^ (ray_odd if p % 2 else ray_even)) * rows + (p ^ pix)))
        return lax.ppermute(value, ("ray", "pix"), moves)

    near = jnp.stack([swap(rays, even, odd) for even, odd in pairs])
    extra = swap(rays, last, last)
    far = swap(near, 0, 0, 1)

    weight = psf_grad.reshape(3, 2, plen // 2, clen)
    weight = jnp.stack([weight[:, 0, ::-1], weight[:, 1]], axis=1).transpose(0, 1, 3, 2)
    if half != plen // 2:
        weight = jnp.pad(weight, ((0, 0), (0, 0), (0, 0), (0, half - plen // 2)))

    chunks = shards * (local // CHUNK)
    sizes = (shards, local, plen, clen, half, count, norm)
    f32, bf16 = jnp.float32, jnp.bfloat16
    vmem = pl.BlockSpec(memory_space=pltpu.VMEM)
    psf, own_sum, near_sum, far_sum, extra_sum = pl.pallas_call(
        functools.partial(psf_kernel, sizes),
        out_shape=[
            jax.ShapeDtypeStruct((3, 2, clen, half), f32),
            jax.ShapeDtypeStruct((4, local), f32),
            jax.ShapeDtypeStruct((count, 4, local), f32),
            jax.ShapeDtypeStruct((count, 4, local), f32),
            jax.ShapeDtypeStruct((4, local), f32),
        ],
        in_specs=[vmem] * 5,
        out_specs=[vmem] * 5,
        scratch_shapes=[
            pltpu.VMEM((6, shards, local), f32),
            pltpu.VMEM((3, 2, local // LANES, 8 * shards, LANES), f32),
            pltpu.VMEM((3, 2, local // LANES, 8 * shards, LANES), f32),
            pltpu.VMEM((3, 4, shards, local), f32),
            pltpu.VMEM((shards, 4, local), f32),
            *[pltpu.VMEM((chunks, 2 * half, CHUNK), bf16)] * 3,
            *[pltpu.VMEM((chunks, 2 * clen, CHUNK), f32)] * 3,
            *[pltpu.VMEM((2 * clen, CHUNK), bf16)] * 3,
            *[pltpu.VMEM((2 * clen, 2 * half), f32)] * 3,
            *[pltpu.VMEM((4 * clen, 2 * half), bf16)] * 3,
        ],
        compiler_params=pltpu.CompilerParams(vmem_limit_bytes=62 * 1024 * 1024),
    )(rays, near, far, extra, weight)

    psf = psf[..., : plen // 2].transpose(0, 1, 3, 2)
    psf = jnp.concatenate([psf[:, 0, ::-1], psf[:, 1]], axis=1)

    near_sum = near_sum + swap(far_sum, 0, 0, 1)
    total = own_sum + swap(extra_sum, last, last)
    for index, (even, odd) in enumerate(pairs):
        total = total + swap(near_sum[index], even, odd)
    bit = 1
    parts = total
    while bit < rows:
        parts = parts + swap(parts, 0, 0, bit)
        bit *= 2
    sums = parts
    grads = jnp.stack(
        [
            sums[0],
            -two_pi * rays[2] * sums[0],
            -two_pi * rays[3] * sums[0],
            (sums[1] - two_pi * rays[0] * sums[0]) / NPIX,
            (sums[2] - two_pi * rays[1] * sums[0]) / NPIX,
            sums[3] / rays[5],
        ]
    )
    return (psf, grads)


def solution(mesh):
    in_specs = (P(None, "ray"), P(None, "ray"), P("ray"), P("ray"), P(None, "pix", "ray"))
    out_specs = (P(None, "pix", "ray"), P(None, "ray"))
    return jax.shard_map(on_device, mesh=mesh, in_specs=in_specs, out_specs=out_specs, check_vma=False)
```

```python
import functools
import math

import jax
import jax.numpy as jnp
from jax import lax
from jax.experimental import pallas as pl
from jax.experimental.pallas import tpu as pltpu
from jax.sharding import PartitionSpec as P

NPIX = 1024
LANES = 128

wave_scales = (1.2088, 1.0, 0.8953)
two_pi = 2.0 * math.pi
sin_terms = [(-1.0) ** n / math.factorial(2 * n + 1) * (0.5 * math.pi) ** (2 * n + 1) for n in range(5)]
cos_terms = [(-1.0) ** n / math.factorial(2 * n) * (0.5 * math.pi) ** (2 * n) for n in range(6)]


def horner(square, terms):
    value = terms[-1]
    for term in terms[-2::-1]:
        value = value * square + term
    return value


def circle(turns):
    rest = turns - jnp.floor(turns + 0.5)
    square = rest * rest
    sin = rest * horner(square, sin_terms)
    cos = horner(square, cos_terms)
    sin, cos = 2.0 * sin * cos, 1.0 - 2.0 * sin * sin
    return 1.0 - 2.0 * sin * sin, 2.0 * sin * cos


def times(left, right):
    return (left[0] * right[0] - left[1] * right[1], left[0] * right[1] + left[1] * right[0])


def ladder(first, second, twice, count):
    out = [first, second]
    while len(out) < count:
        out.append(twice * out[-1] - out[-2])
    return out[:count]


def climb(first, second, twice, count):
    re = ladder(first[0], second[0], twice, count)
    im = ladder(first[1], second[1], twice, count)
    return list(zip(re, im))


def psf_kernel(sizes, *refs):
    count = sizes[0]
    ray_refs, grad_ref, psf_ref, sum_refs = refs[:count], refs[count], refs[count + 1], refs[count + 2 : 2 * count + 2]
    (rays_s, dense, row_fine, row_wide, col_base, col_step, grad_s, psf_s, cot_t, sums, ray_sem, grad_sem, psf_sem,
     *tables) = refs[2 * count + 2 :]
    shards, local, plen, clen, wides, norm = sizes
    wide_clen = max(clen, LANES)
    tiles = local // LANES
    row_tab, col_tab, col_half, field, cot = [tables[3 * n : 3 * n + 3] for n in range(5)]

    loads = []

    def load(source, slot):
        loads.append(pltpu.make_async_copy(source, rays_s.at[slot], ray_sem.at[slot]))
        loads[-1].start()

    for slot in range(shards):
        load(ray_refs[slot], slot)
    grad_load = pltpu.make_async_copy(grad_ref, grad_s, grad_sem)
    grad_load.start()

    x_mid = (lax.axis_index("pix") * plen).astype(jnp.float32) + (0.5 * plen - 0.5 * NPIX)
    y_low = (lax.axis_index("ray") * clen).astype(jnp.float32) + (0.5 - 0.5 * NPIX)
    for wave in range(3):
        field[wave][...] = jnp.zeros_like(field[wave])
        if wide_clen > clen:
            col_half[wave][...] = jnp.zeros_like(col_half[wave])
    for slot, copy in enumerate(loads):
        copy.wait()
        for tile in range(tiles):
            for item in range(4):
                dense[item, tile, slot : slot + 1, :] = rays_s[slot, tile, item : item + 1, :]

    @pl.loop(0, tiles)
    def _(tile):
        path, dir_l, dir_m, amp = [dense[item, tile] for item in range(4)]
        phase = path + (dir_l * x_mid + dir_m * y_low)
        amp = amp * norm

        def spread(base, values):
            for sub, value in enumerate(values):
                for part in range(2):
                    base[wave, part, tile, pl.ds(sub, shards, stride=8), :] = value[part]

        for wave in range(3):
            scale = wave_scales[wave]
            first = circle((0.5 * scale) * dir_l)
            step = times(first, first)
            spread(row_fine, climb(first, times(first, step), 2.0 * step[0], 8))
            first = circle((8.0 * scale) * dir_l)
            step = times(first, first)
            spread(row_wide, climb(first, times(first, step), 2.0 * step[0], wides))
            cos, sin = circle(scale * phase)
            first = (amp * cos, amp * sin)
            step = circle(scale * dir_m)
            spread(col_base, climb(first, times(first, step), 2.0 * step[0], 8))
            step = circle((8.0 * scale) * dir_m)
            for index, value in enumerate((step[0], step[1], 2.0 * step[0])):
                col_step[wave, index, tile, :shards, :] = value

    @pl.loop(0, shards)
    def _(shard):
        rows8 = pl.ds(pl.multiple_of(shard * 8, 8), 8)
        for wave in range(3):
            def whole(ref, *index):
                return jnp.concatenate([ref[(wave, index[0], tile) + index[1:]] for tile in range(tiles)], axis=1)

            every = slice(None)
            fine = [whole(row_fine, part, rows8, every) for part in range(2)]
            for pair in range(wides // 2):
                wide = [[whole(row_wide, part, pl.ds(shard * 8 + 2 * pair + n, 8, stride=0), every) for n in range(2)] for part in range(2)]
                for wide_part, fine_part, block in ((0, 0, 0), (1, 1, 1), (1, 0, 2), (0, 1, 3)):
                    both = [wide[wide_part][n] * fine[fine_part] for n in range(2)]
                    rows16 = slice(8 * wides * block + 16 * pair, 8 * wides * block + 16 * pair + 16)
                    row_tab[wave][shard, rows16, :] = jnp.concatenate(both, axis=0).astype(jnp.bfloat16)
            step = [whole(col_step, index, pl.ds(shard, 8, stride=0), every) for index in range(3)]
            first = [whole(col_base, part, rows8, every) for part in range(2)]
            second = times(first, step)
            for part in range(2):
                run = ladder(first[part], second[part], step[2], clen // 8)
                for pair in range(clen // 16):
                    both = jnp.concatenate(run[2 * pair : 2 * pair + 2], axis=0)
                    rows16 = slice(part * clen + 16 * pair, part * clen + 16 * pair + 16)
                    col_tab[wave][shard, rows16, :] = both
                    low = part * wide_clen + 16 * pair
                    col_half[wave][low : low + 16, :] = both.astype(jnp.bfloat16)
            field[wave][...] += lax.dot_general(
                row_tab[wave][shard], col_half[wave][...], (((1,), (1,)), ((), ())), preferred_element_type=jnp.float32
            )

    sub8 = lax.broadcasted_iota(jnp.int32, (8, wide_clen), 0)
    fine_row = sub8.astype(jnp.float32) + 0.5
    mid = plen // 2

    def flip(value):
        return jnp.take_along_axis(value, 7 - sub8, axis=0)

    grad_load.wait()
    for wave in range(3):
        for wide in range(wides):
            parts = []
            for side in (slice(0, wide_clen), slice(wide_clen, 2 * wide_clen)):
                parts.append([field[wave][8 * (wides * block + wide) : 8 * (wides * block + wide) + 8, side] for block in range(4)])
            (cc_r, ss_r, sc_r, cs_r), (cc_i, ss_i, sc_i, cs_i) = parts
            lines = []
            for sign in (1, -1):
                if sign == 1:
                    even_r, even_i, odd_r, odd_i = cc_r - ss_r, cc_i - ss_i, sc_r + cs_r, sc_i + cs_i
                    up_row, dn_row = mid + 16 * wide + 8, mid - 16 * wide - 16
                    offset = (16.0 * wide + 8.0) + fine_row
                else:
                    even_r, even_i, odd_r, odd_i = cc_r + ss_r, cc_i + ss_i, sc_r - cs_r, sc_i - cs_i
                    up_row, dn_row = mid + 16 * wide, mid - 16 * wide - 8
                    offset = (16.0 * wide + 8.0) - fine_row
                up_r, up_i = even_r - odd_i, even_i + odd_r
                dn_r, dn_i = even_r + odd_i, even_i - odd_r
                up_rows, dn_rows = slice(up_row, up_row + 8), slice(dn_row, dn_row + 8)
                up, dn = up_r * up_r + up_i * up_i, dn_r * dn_r + dn_i * dn_i
                g_up, g_dn = grad_s[wave, up_rows, :], grad_s[wave, dn_rows, :]
                if sign == 1:
                    dn, g_dn = flip(dn), flip(g_dn)
                else:
                    up, g_up = flip(up), flip(g_up)
                psf_s[wave, up_rows, :] = up
                psf_s[wave, dn_rows, :] = dn
                dn_r, dn_i, up_r, up_i = g_dn * dn_r, g_dn * dn_i, g_up * up_r, g_up * up_i
                p_r, p_i, m_r, m_i = up_r + dn_r, up_i + dn_i, up_r - dn_r, up_i - dn_i
                lines.append(
                    ((p_r, m_i), (p_i, -m_r), (offset * m_r, offset * p_i), (offset * m_i, -(offset * p_r)))
                )
            for kind in range(4):
                (cos_p, sin_p), (cos_m, sin_m) = lines[0][kind], lines[1][kind]
                for block, value in enumerate((cos_p + cos_m, cos_m - cos_p, sin_p + sin_m, sin_p - sin_m)):
                    cot_t[kind, 8 * (wides * block + wide) : 8 * (wides * block + wide) + 8, :] = value
        flat = [cot_t[kind].T for kind in range(4)]
        for group in range(clen // 8):
            rows = slice(8 * group, 8 * group + 8)
            for pair in range(2):
                both = jnp.concatenate([flat[2 * pair][rows], flat[2 * pair + 1][rows]], axis=0)
                cot[wave][32 * group + 16 * pair : 32 * group + 16 * pair + 16, :] = both.astype(jnp.bfloat16)
    psf_store = pltpu.make_async_copy(psf_s, psf_ref, psf_sem)
    psf_store.start()

    sub = lax.broadcasted_iota(jnp.int32, (8, local), 0).astype(jnp.float32)
    y_sub = sub + (y_low + clen)

    @pl.loop(0, shards)
    def _(shard):
        total = [jnp.zeros((8, local), jnp.float32) for _ in range(4)]
        for wave in range(3):
            scale = 2.0 * wave_scales[wave]
            back = jnp.dot(cot[wave][...], row_tab[wave][shard], preferred_element_type=jnp.float32)
            im_sum = jnp.zeros((8, local), jnp.float32)
            up_sum = jnp.zeros((8, local), jnp.float32)
            re_sum = jnp.zeros((8, local), jnp.float32)
            x_sum = jnp.zeros((8, local), jnp.float32)
            for group in range(clen // 8):
                e_r, e_i, f_r, f_i = [back[32 * group + 8 * n : 32 * group + 8 * n + 8] for n in range(4)]
                b_r = col_tab[wave][shard, 8 * group : 8 * group + 8, :]
                b_i = col_tab[wave][shard, clen + 8 * group : clen + 8 * group + 8, :]
                im_sum = im_sum + (b_r * e_i - b_i * e_r)
                re_sum = re_sum + (b_r * e_r + b_i * e_i)
                x_sum = x_sum + (b_r * f_i - b_i * f_r)
                up_sum = up_sum + im_sum
            total[0] = total[0] + scale * im_sum
            total[1] = total[1] + (scale * two_pi) * (x_mid * im_sum + x_sum)
            total[2] = total[2] + (scale * two_pi) * (y_sub * im_sum - 8.0 * up_sum)
            total[3] = total[3] + 2.0 * re_sum
        rows = [jnp.sum(value, axis=0, keepdims=True) for value in total]
        sums[shard] = jnp.concatenate(rows, axis=0)

    for slot in range(shards):
        sum_refs[slot][...] = sums[slot]
    psf_store.wait()


def split_pairs(shards):
    if shards == 8:
        return ((2, 7), (4, 5), (3, 6)), 1
    pairs = (shards - 2) // 2
    return tuple((1 + n, 1 + pairs + n) for n in range(pairs)), shards - 1


def on_device(positions, directions, path, amplitude, psf_grad):
    x, y, dir_l, dir_m = positions[0], positions[1], directions[0], directions[1]
    local = path.shape[0]
    tiles = local // LANES
    shards = lax.axis_size("ray")
    rows = lax.axis_size("pix")
    plen = NPIX // rows
    clen = NPIX // shards
    wides = plen // 32
    wide_clen = max(clen, LANES)
    norm = 1.0 / math.sqrt(local * shards)
    pairs, last = split_pairs(shards)
    count = len(pairs)

    def swap(value, ray_even, ray_odd, pix=0):
        moves = []
        for r in range(shards):
            for p in range(rows):
                moves.append((r * rows + p, (r ^ (ray_odd if p % 2 else ray_even)) * rows + (p ^ pix)))
        return lax.ppermute(value, ("ray", "pix"), moves)

    fixed = path * (1.0 / two_pi) - (dir_l * x + dir_m * y)
    packed = jnp.stack([fixed, dir_l, dir_m, amplitude]).reshape(4, tiles, LANES).transpose(1, 0, 2)
    near = [swap(packed, even, odd) for even, odd in pairs]
    extra = swap(packed, last, last)
    far = [swap(part, 0, 0, 1) for part in near]

    weight = jnp.pad(psf_grad, ((0, 0), (0, 0), (0, wide_clen - clen))) if wide_clen > clen else psf_grad
    sizes = (shards, local, plen, clen, wides, norm)
    f32, bf16 = jnp.float32, jnp.bfloat16
    vmem = pl.BlockSpec(memory_space=pltpu.VMEM)
    anywhere = pl.BlockSpec(memory_space=pltpu.HBM)
    psf, *parts = pl.pallas_call(
        functools.partial(psf_kernel, sizes),
        out_shape=[jax.ShapeDtypeStruct((3, plen, wide_clen), f32)] + [jax.ShapeDtypeStruct((4, local), f32)] * shards,
        in_specs=[anywhere] * (shards + 1),
        out_specs=[anywhere] + [vmem] * shards,
        scratch_shapes=[
            pltpu.VMEM((shards, tiles, 4, LANES), f32),
            pltpu.VMEM((4, tiles, shards, LANES), f32),
            pltpu.VMEM((3, 2, tiles, 8 * shards, LANES), f32),
            pltpu.VMEM((3, 2, tiles, 8 * shards + 8, LANES), f32),
            pltpu.VMEM((3, 2, tiles, 8 * shards, LANES), f32),
            pltpu.VMEM((3, 3, tiles, shards + 8, LANES), f32),
            pltpu.VMEM((3, plen, wide_clen), f32),
            pltpu.VMEM((3, plen, wide_clen), f32),
            pltpu.VMEM((4, 32 * wides, wide_clen), f32),
            pltpu.VMEM((shards, 4, local), f32),
            pltpu.SemaphoreType.DMA((shards,)),
            pltpu.SemaphoreType.DMA,
            pltpu.SemaphoreType.DMA,
            *[pltpu.VMEM((shards, 32 * wides, local), bf16)] * 3,
            *[pltpu.VMEM((shards, 2 * clen, local), f32)] * 3,
            *[pltpu.VMEM((2 * wide_clen, local), bf16)] * 3,
            *[pltpu.VMEM((32 * wides, 2 * wide_clen), f32)] * 3,
            *[pltpu.VMEM((4 * clen, 32 * wides), bf16)] * 3,
        ],
        compiler_params=pltpu.CompilerParams(vmem_limit_bytes=62 * 1024 * 1024),
    )(packed, *near, *far, extra, weight)

    psf = psf[..., :clen]

    own_sum, near_sum, far_sum, extra_sum = parts[0], parts[1 : 1 + count], parts[1 + count : 1 + 2 * count], parts[-1]
    near_sum = [near + swap(far, 0, 0, 1) for near, far in zip(near_sum, far_sum)]
    total = own_sum + swap(extra_sum, last, last)
    for part, (even, odd) in zip(near_sum, pairs):
        total = total + swap(part, even, odd)
    bit = 1
    while bit < rows:
        total = total + swap(total, 0, 0, bit)
        bit *= 2
    s1, s2, s3, s4 = total
    grads = jnp.stack(
        [
            s1,
            -two_pi * dir_l * s1,
            -two_pi * dir_m * s1,
            (s2 - two_pi * x * s1) / NPIX,
            (s3 - two_pi * y * s1) / NPIX,
            s4 / amplitude,
        ]
    )
    return (psf, grads)


def solution(mesh):
    in_specs = (P(None, "ray"), P(None, "ray"), P("ray"), P("ray"), P(None, "pix", "ray"))
    out_specs = (P(None, "pix", "ray"), P(None, "ray"))
    return jax.shard_map(on_device, mesh=mesh, in_specs=in_specs, out_specs=out_specs, check_vma=False)
```

```python
import functools
import math

import jax
import jax.numpy as jnp
from jax import lax
from jax.experimental import pallas as pl
from jax.experimental.pallas import tpu as pltpu
from jax.sharding import PartitionSpec as P

NPIX = 1024
LANES = 128

wave_scales = (1.2088, 1.0, 0.8953)
two_pi = 2.0 * math.pi
sin_terms = [(-1.0) ** n / math.factorial(2 * n + 1) * (0.5 * math.pi) ** (2 * n + 1) for n in range(5)]
cos_terms = [(-1.0) ** n / math.factorial(2 * n) * (0.5 * math.pi) ** (2 * n) for n in range(6)]


def horner(square, terms):
    value = terms[-1]
    for term in terms[-2::-1]:
        value = value * square + term
    return value


def circle(turns):
    rest = turns - jnp.floor(turns + 0.5)
    square = rest * rest
    sin = rest * horner(square, sin_terms)
    cos = horner(square, cos_terms)
    sin, cos = 2.0 * sin * cos, 1.0 - 2.0 * sin * sin
    return 1.0 - 2.0 * sin * sin, 2.0 * sin * cos


def times(left, right):
    return (left[0] * right[0] - left[1] * right[1], left[0] * right[1] + left[1] * right[0])


def ladder(first, second, twice, count):
    out = [first, second]
    while len(out) < count:
        out.append(twice * out[-1] - out[-2])
    return out[:count]


def climb(first, second, twice, count):
    re = ladder(first[0], second[0], twice, count)
    im = ladder(first[1], second[1], twice, count)
    return list(zip(re, im))


def psf_kernel(sizes, *refs):
    count = sizes[0]
    ray_refs, grad_ref, psf_ref, sum_refs = refs[:count], refs[count], refs[count + 1], refs[count + 2 : 2 * count + 2]
    (rays_s, dense, row_fine, row_wide, col_base, col_step, grad_s, psf_s, cot_t, sums, ray_sem, grad_sem, psf_sem,
     *tables) = refs[2 * count + 2 :]
    shards, local, plen, clen, wides, norm = sizes
    wide_clen = max(clen, LANES)
    tiles = local // LANES
    row_tab, col_tab, col_half, field, cot = [tables[3 * n : 3 * n + 3] for n in range(5)]

    loads = []

    def load(source, slot):
        loads.append(pltpu.make_async_copy(source, rays_s.at[slot], ray_sem.at[slot]))
        loads[-1].start()

    for slot in range(shards):
        load(ray_refs[slot], slot)
    grad_load = pltpu.make_async_copy(grad_ref, grad_s, grad_sem)
    grad_load.start()

    x_mid = (lax.axis_index("pix") * plen).astype(jnp.float32) + (0.5 * plen - 0.5 * NPIX)
    y_low = (lax.axis_index("ray") * clen).astype(jnp.float32) + (0.5 - 0.5 * NPIX)
    for wave in range(3):
        field[wave][...] = jnp.zeros_like(field[wave])
        if wide_clen > clen:
            col_half[wave][...] = jnp.zeros_like(col_half[wave])
    for slot, copy in enumerate(loads):
        copy.wait()
        for tile in range(tiles):
            for item in range(4):
                dense[item, tile, slot : slot + 1, :] = rays_s[slot, tile, item : item + 1, :]

    @pl.loop(0, tiles, unroll=True)
    def _(tile):
        path, dir_l, dir_m, amp = [dense[item, tile] for item in range(4)]
        phase = path + (dir_l * x_mid + dir_m * y_low)
        amp = amp * norm

        def spread(base, values):
            for sub, value in enumerate(values):
                for part in range(2):
                    base[wave, part, tile, pl.ds(sub, shards, stride=8), :] = value[part]

        for wave in range(3):
            scale = wave_scales[wave]
            first = circle((0.5 * scale) * dir_l)
            step = times(first, first)
            spread(row_fine, climb(first, times(first, step), 2.0 * step[0], 8))
            first = circle((8.0 * scale) * dir_l)
            step = times(first, first)
            spread(row_wide, climb(first, times(first, step), 2.0 * step[0], wides))
            cos, sin = circle(scale * phase)
            first = (amp * cos, amp * sin)
            step = circle(scale * dir_m)
            spread(col_base, climb(first, times(first, step), 2.0 * step[0], 8))
            step = circle((8.0 * scale) * dir_m)
            for index, value in enumerate((step[0], step[1], 2.0 * step[0])):
                col_step[wave, index, tile, :shards, :] = value

    @pl.loop(0, shards)
    def _(shard):
        rows8 = pl.ds(pl.multiple_of(shard * 8, 8), 8)
        for wave in range(3):
            def whole(ref, *index):
                return jnp.concatenate([ref[(wave, index[0], tile) + index[1:]] for tile in range(tiles)], axis=1)

            every = slice(None)
            fine = [whole(row_fine, part, rows8, every) for part in range(2)]
            for pair in range(wides // 2):
                wide = [[whole(row_wide, part, pl.ds(shard * 8 + 2 * pair + n, 8, stride=0), every) for n in range(2)] for part in range(2)]
                for wide_part, fine_part, block in ((0, 0, 0), (1, 1, 1), (1, 0, 2), (0, 1, 3)):
                    both = [wide[wide_part][n] * fine[fine_part] for n in range(2)]
                    rows16 = slice(8 * wides * block + 16 * pair, 8 * wides * block + 16 * pair + 16)
                    row_tab[wave][shard, rows16, :] = jnp.concatenate(both, axis=0).astype(jnp.bfloat16)
            step = [whole(col_step, index, pl.ds(shard, 8, stride=0), every) for index in range(3)]
            first = [whole(col_base, part, rows8, every) for part in range(2)]
            second = times(first, step)
            for part in range(2):
                run = ladder(first[part], second[part], step[2], clen // 8)
                for pair in range(clen // 16):
                    both = jnp.concatenate(run[2 * pair : 2 * pair + 2], axis=0)
                    rows16 = slice(part * clen + 16 * pair, part * clen + 16 * pair + 16)
                    col_tab[wave][shard, rows16, :] = both
                    low = part * wide_clen + 16 * pair
                    col_half[wave][low : low + 16, :] = both.astype(jnp.bfloat16)
            field[wave][...] += lax.dot_general(
                row_tab[wave][shard], col_half[wave][...], (((1,), (1,)), ((), ())), preferred_element_type=jnp.float32
            )

    sub8 = lax.broadcasted_iota(jnp.int32, (8, wide_clen), 0)
    fine_row = sub8.astype(jnp.float32) + 0.5
    mid = plen // 2

    def flip(value):
        return jnp.take_along_axis(value, 7 - sub8, axis=0)

    grad_load.wait()
    for wave in range(3):
        for wide in range(wides):
            parts = []
            for side in (slice(0, wide_clen), slice(wide_clen, 2 * wide_clen)):
                parts.append([field[wave][8 * (wides * block + wide) : 8 * (wides * block + wide) + 8, side] for block in range(4)])
            (cc_r, ss_r, sc_r, cs_r), (cc_i, ss_i, sc_i, cs_i) = parts
            lines = []
            for sign in (1, -1):
                if sign == 1:
                    even_r, even_i, odd_r, odd_i = cc_r - ss_r, cc_i - ss_i, sc_r + cs_r, sc_i + cs_i
                    up_row, dn_row = mid + 16 * wide + 8, mid - 16 * wide - 16
                    offset = (16.0 * wide + 8.0) + fine_row
                else:
                    even_r, even_i, odd_r, odd_i = cc_r + ss_r, cc_i + ss_i, sc_r - cs_r, sc_i - cs_i
                    up_row, dn_row = mid + 16 * wide, mid - 16 * wide - 8
                    offset = (16.0 * wide + 8.0) - fine_row
                up_r, up_i = even_r - odd_i, even_i + odd_r
                dn_r, dn_i = even_r + odd_i, even_i - odd_r
                up_rows, dn_rows = slice(up_row, up_row + 8), slice(dn_row, dn_row + 8)
                up, dn = up_r * up_r + up_i * up_i, dn_r * dn_r + dn_i * dn_i
                g_up, g_dn = grad_s[wave, up_rows, :], grad_s[wave, dn_rows, :]
                if sign == 1:
                    dn, g_dn = flip(dn), flip(g_dn)
                else:
                    up, g_up = flip(up), flip(g_up)
                psf_s[wave, up_rows, :] = up
                psf_s[wave, dn_rows, :] = dn
                dn_r, dn_i, up_r, up_i = g_dn * dn_r, g_dn * dn_i, g_up * up_r, g_up * up_i
                p_r, p_i, m_r, m_i = up_r + dn_r, up_i + dn_i, up_r - dn_r, up_i - dn_i
                lines.append(
                    ((p_r, m_i), (p_i, -m_r), (offset * m_r, offset * p_i), (offset * m_i, -(offset * p_r)))
                )
            for kind in range(4):
                (cos_p, sin_p), (cos_m, sin_m) = lines[0][kind], lines[1][kind]
                for block, value in enumerate((cos_p + cos_m, cos_m - cos_p, sin_p + sin_m, sin_p - sin_m)):
                    cot_t[kind, 8 * (wides * block + wide) : 8 * (wides * block + wide) + 8, :] = value
        flat = [cot_t[kind].T for kind in range(4)]
        for group in range(clen // 8):
            rows = slice(8 * group, 8 * group + 8)
            for pair in range(2):
                both = jnp.concatenate([flat[2 * pair][rows], flat[2 * pair + 1][rows]], axis=0)
                cot[wave][32 * group + 16 * pair : 32 * group + 16 * pair + 16, :] = both.astype(jnp.bfloat16)
    psf_store = pltpu.make_async_copy(psf_s, psf_ref, psf_sem)
    psf_store.start()

    sub = lax.broadcasted_iota(jnp.int32, (8, local), 0).astype(jnp.float32)
    y_sub = sub + (y_low + clen)

    @pl.loop(0, shards)
    def _(shard):
        total = [jnp.zeros((8, local), jnp.float32) for _ in range(4)]
        for wave in range(3):
            scale = 2.0 * wave_scales[wave]
            back = jnp.dot(cot[wave][...], row_tab[wave][shard], preferred_element_type=jnp.float32)
            im_sum = jnp.zeros((8, local), jnp.float32)
            up_sum = jnp.zeros((8, local), jnp.float32)
            re_sum = jnp.zeros((8, local), jnp.float32)
            x_sum = jnp.zeros((8, local), jnp.float32)
            for group in range(clen // 8):
                e_r, e_i, f_r, f_i = [back[32 * group + 8 * n : 32 * group + 8 * n + 8] for n in range(4)]
                b_r = col_tab[wave][shard, 8 * group : 8 * group + 8, :]
                b_i = col_tab[wave][shard, clen + 8 * group : clen + 8 * group + 8, :]
                im_sum = im_sum + (b_r * e_i - b_i * e_r)
                re_sum = re_sum + (b_r * e_r + b_i * e_i)
                x_sum = x_sum + (b_r * f_i - b_i * f_r)
                up_sum = up_sum + im_sum
            total[0] = total[0] + scale * im_sum
            total[1] = total[1] + (scale * two_pi) * (x_mid * im_sum + x_sum)
            total[2] = total[2] + (scale * two_pi) * (y_sub * im_sum - 8.0 * up_sum)
            total[3] = total[3] + 2.0 * re_sum
        rows = [jnp.sum(value, axis=0, keepdims=True) for value in total]
        sums[shard] = jnp.concatenate(rows, axis=0)

    for slot in range(shards):
        sum_refs[slot][...] = sums[slot]
    psf_store.wait()


def split_pairs(shards):
    if shards == 8:
        return ((3, 7), (4, 5), (1, 6)), 2
    pairs = (shards - 2) // 2
    return tuple((1 + n, 1 + pairs + n) for n in range(pairs)), shards - 1


def on_device(positions, directions, path, amplitude, psf_grad):
    x, y, dir_l, dir_m = positions[0], positions[1], directions[0], directions[1]
    local = path.shape[0]
    tiles = local // LANES
    shards = lax.axis_size("ray")
    rows = lax.axis_size("pix")
    plen = NPIX // rows
    clen = NPIX // shards
    wides = plen // 32
    wide_clen = max(clen, LANES)
    norm = 1.0 / math.sqrt(local * shards)
    pairs, last = split_pairs(shards)
    count = len(pairs)

    def swap(value, ray_even, ray_odd, pix=0):
        moves = []
        for r in range(shards):
            for p in range(rows):
                moves.append((r * rows + p, (r ^ (ray_odd if p % 2 else ray_even)) * rows + (p ^ pix)))
        return lax.ppermute(value, ("ray", "pix"), moves)

    fixed = path * (1.0 / two_pi) - (dir_l * x + dir_m * y)
    packed = jnp.stack([fixed, dir_l, dir_m, amplitude]).reshape(4, tiles, LANES).transpose(1, 0, 2)
    near = [swap(packed, even, odd) for even, odd in pairs]
    extra = swap(packed, last, last)
    far = [swap(part, 0, 0, 1) for part in near]

    weight = jnp.pad(psf_grad, ((0, 0), (0, 0), (0, wide_clen - clen))) if wide_clen > clen else psf_grad
    sizes = (shards, local, plen, clen, wides, norm)
    f32, bf16 = jnp.float32, jnp.bfloat16
    vmem = pl.BlockSpec(memory_space=pltpu.VMEM)
    anywhere = pl.BlockSpec(memory_space=pltpu.HBM)
    psf, *parts = pl.pallas_call(
        functools.partial(psf_kernel, sizes),
        out_shape=[jax.ShapeDtypeStruct((3, plen, wide_clen), f32)] + [jax.ShapeDtypeStruct((4, local), f32)] * shards,
        in_specs=[anywhere] * (shards + 1),
        out_specs=[anywhere] + [vmem] * shards,
        scratch_shapes=[
            pltpu.VMEM((shards, tiles, 4, LANES), f32),
            pltpu.VMEM((4, tiles, shards, LANES), f32),
            pltpu.VMEM((3, 2, tiles, 8 * shards, LANES), f32),
            pltpu.VMEM((3, 2, tiles, 8 * shards + 8, LANES), f32),
            pltpu.VMEM((3, 2, tiles, 8 * shards, LANES), f32),
            pltpu.VMEM((3, 3, tiles, shards + 8, LANES), f32),
            pltpu.VMEM((3, plen, wide_clen), f32),
            pltpu.VMEM((3, plen, wide_clen), f32),
            pltpu.VMEM((4, 32 * wides, wide_clen), f32),
            pltpu.VMEM((shards, 4, local), f32),
            pltpu.SemaphoreType.DMA((shards,)),
            pltpu.SemaphoreType.DMA,
            pltpu.SemaphoreType.DMA,
            *[pltpu.VMEM((shards, 32 * wides, local), bf16)] * 3,
            *[pltpu.VMEM((shards, 2 * clen, local), f32)] * 3,
            *[pltpu.VMEM((2 * wide_clen, local), bf16)] * 3,
            *[pltpu.VMEM((32 * wides, 2 * wide_clen), f32)] * 3,
            *[pltpu.VMEM((4 * clen, 32 * wides), bf16)] * 3,
        ],
        compiler_params=pltpu.CompilerParams(vmem_limit_bytes=62 * 1024 * 1024),
    )(packed, *near, *far, extra, weight)

    psf = psf[..., :clen]

    own_sum, near_sum, far_sum, extra_sum = parts[0], parts[1 : 1 + count], parts[1 + count : 1 + 2 * count], parts[-1]
    near_sum = [near + swap(far, 0, 0, 1) for near, far in zip(near_sum, far_sum)]
    total = own_sum + swap(extra_sum, last, last)
    for part, (even, odd) in zip(near_sum, pairs):
        total = total + swap(part, even, odd)
    bit = rows // 2
    while bit:
        total = total + swap(total, 0, 0, bit)
        bit //= 2
    s1, s2, s3, s4 = total
    grads = jnp.stack(
        [
            s1,
            -two_pi * dir_l * s1,
            -two_pi * dir_m * s1,
            (s2 - two_pi * x * s1) / NPIX,
            (s3 - two_pi * y * s1) / NPIX,
            s4 / amplitude,
        ]
    )
    return (psf, grads)


def solution(mesh):
    in_specs = (P(None, "ray"), P(None, "ray"), P("ray"), P("ray"), P(None, "pix", "ray"))
    out_specs = (P(None, "pix", "ray"), P(None, "ray"))
    return jax.shard_map(on_device, mesh=mesh, in_specs=in_specs, out_specs=out_specs, check_vma=False)
```

```python
import functools
import math

import jax
import jax.numpy as jnp
from jax import lax
from jax.experimental import pallas as pl
from jax.experimental.pallas import tpu as pltpu
from jax.sharding import PartitionSpec as P

NPIX = 1024
LANES = 128

wave_scales = (1.2088, 1.0, 0.8953)
two_pi = 2.0 * math.pi
sin_terms = [(-1.0) ** n / math.factorial(2 * n + 1) * (0.5 * math.pi) ** (2 * n + 1) for n in range(5)]
cos_terms = [(-1.0) ** n / math.factorial(2 * n) * (0.5 * math.pi) ** (2 * n) for n in range(6)]


def horner(square, terms):
    value = terms[-1]
    for term in terms[-2::-1]:
        value = value * square + term
    return value


def circle(turns):
    rest = turns - jnp.floor(turns + 0.5)
    square = rest * rest
    sin = rest * horner(square, sin_terms)
    cos = horner(square, cos_terms)
    sin, cos = 2.0 * sin * cos, 1.0 - 2.0 * sin * sin
    return 1.0 - 2.0 * sin * sin, 2.0 * sin * cos


def times(left, right):
    return (left[0] * right[0] - left[1] * right[1], left[0] * right[1] + left[1] * right[0])


def ladder(first, second, twice, count):
    out = [first, second]
    while len(out) < count:
        out.append(twice * out[-1] - out[-2])
    return out[:count]


def climb(first, second, twice, count):
    re = ladder(first[0], second[0], twice, count)
    im = ladder(first[1], second[1], twice, count)
    return list(zip(re, im))


def psf_kernel(sizes, *refs):
    count = sizes[0]
    ray_refs, grad_ref, psf_ref, sum_refs = refs[:count], refs[count], refs[count + 1], refs[count + 2 : 2 * count + 2]
    (rays_s, dense, row_fine, row_wide, col_base, col_step, grad_s, psf_s, cot_t, sums, ray_sem, grad_sem, psf_sem,
     *tables) = refs[2 * count + 2 :]
    shards, local, plen, clen, wides, norm = sizes
    wide_clen = max(clen, LANES)
    tiles = local // LANES
    row_tab, col_tab, col_half, field, cot = [tables[3 * n : 3 * n + 3] for n in range(5)]

    loads = []

    def load(source, slot):
        loads.append(pltpu.make_async_copy(source, rays_s.at[slot], ray_sem.at[slot]))
        loads[-1].start()

    for slot in range(shards):
        load(ray_refs[slot], slot)
    grad_load = pltpu.make_async_copy(grad_ref, grad_s, grad_sem)
    grad_load.start()

    x_mid = (lax.axis_index("pix") * plen).astype(jnp.float32) + (0.5 * plen - 0.5 * NPIX)
    y_low = (lax.axis_index("ray") * clen).astype(jnp.float32) + (0.5 - 0.5 * NPIX)
    for wave in range(3):
        field[wave][...] = jnp.zeros_like(field[wave])
        if wide_clen > clen:
            col_half[wave][...] = jnp.zeros_like(col_half[wave])
    for slot, copy in enumerate(loads):
        copy.wait()
        for tile in range(tiles):
            for item in range(4):
                dense[item, tile, slot : slot + 1, :] = rays_s[slot, tile, item : item + 1, :]

    @pl.loop(0, tiles, unroll=True)
    def _(tile):
        path, dir_l, dir_m, amp = [dense[item, tile] for item in range(4)]
        phase = path + (dir_l * x_mid + dir_m * y_low)
        amp = amp * norm

        def spread(base, values):
            for sub, value in enumerate(values):
                for part in range(2):
                    base[wave, part, tile, pl.ds(sub, shards, stride=8), :] = value[part]

        for wave in range(3):
            scale = wave_scales[wave]
            first = circle((0.5 * scale) * dir_l)
            step = times(first, first)
            spread(row_fine, climb(first, times(first, step), 2.0 * step[0], 8))
            first = circle((8.0 * scale) * dir_l)
            step = times(first, first)
            spread(row_wide, climb(first, times(first, step), 2.0 * step[0], wides))
            cos, sin = circle(scale * phase)
            first = (amp * cos, amp * sin)
            step = circle(scale * dir_m)
            spread(col_base, climb(first, times(first, step), 2.0 * step[0], 8))
            step = circle((8.0 * scale) * dir_m)
            for index, value in enumerate((step[0], step[1], 2.0 * step[0])):
                col_step[wave, index, tile, :shards, :] = value

    @pl.loop(0, shards)
    def _(shard):
        rows8 = pl.ds(pl.multiple_of(shard * 8, 8), 8)
        for wave in range(3):
            def whole(ref, *index):
                return jnp.concatenate([ref[(wave, index[0], tile) + index[1:]] for tile in range(tiles)], axis=1)

            every = slice(None)
            fine = [whole(row_fine, part, rows8, every) for part in range(2)]
            for pair in range(wides // 2):
                wide = [[whole(row_wide, part, pl.ds(shard * 8 + 2 * pair + n, 8, stride=0), every) for n in range(2)] for part in range(2)]
                for wide_part, fine_part, block in ((0, 0, 0), (1, 1, 1), (1, 0, 2), (0, 1, 3)):
                    both = [wide[wide_part][n] * fine[fine_part] for n in range(2)]
                    rows16 = slice(8 * wides * block + 16 * pair, 8 * wides * block + 16 * pair + 16)
                    row_tab[wave][shard, rows16, :] = jnp.concatenate(both, axis=0).astype(jnp.bfloat16)
            step = [whole(col_step, index, pl.ds(shard, 8, stride=0), every) for index in range(3)]
            first = [whole(col_base, part, rows8, every) for part in range(2)]
            second = times(first, step)
            for part in range(2):
                run = ladder(first[part], second[part], step[2], clen // 8)
                for pair in range(clen // 16):
                    both = jnp.concatenate(run[2 * pair : 2 * pair + 2], axis=0)
                    rows16 = slice(part * clen + 16 * pair, part * clen + 16 * pair + 16)
                    col_tab[wave][shard, rows16, :] = both
                    low = part * wide_clen + 16 * pair
                    col_half[wave][low : low + 16, :] = both.astype(jnp.bfloat16)
            field[wave][...] += lax.dot_general(
                row_tab[wave][shard], col_half[wave][...], (((1,), (1,)), ((), ())), preferred_element_type=jnp.float32
            )

    sub8 = lax.broadcasted_iota(jnp.int32, (8, wide_clen), 0)
    fine_row = sub8.astype(jnp.float32) + 0.5
    mid = plen // 2

    def flip(value):
        return jnp.take_along_axis(value, 7 - sub8, axis=0)

    grad_load.wait()
    for wave in range(3):
        for wide in range(wides):
            parts = []
            for side in (slice(0, wide_clen), slice(wide_clen, 2 * wide_clen)):
                parts.append([field[wave][8 * (wides * block + wide) : 8 * (wides * block + wide) + 8, side] for block in range(4)])
            (cc_r, ss_r, sc_r, cs_r), (cc_i, ss_i, sc_i, cs_i) = parts
            lines = []
            for sign in (1, -1):
                if sign == 1:
                    even_r, even_i, odd_r, odd_i = cc_r - ss_r, cc_i - ss_i, sc_r + cs_r, sc_i + cs_i
                    up_row, dn_row = mid + 16 * wide + 8, mid - 16 * wide - 16
                    offset = (16.0 * wide + 8.0) + fine_row
                else:
                    even_r, even_i, odd_r, odd_i = cc_r + ss_r, cc_i + ss_i, sc_r - cs_r, sc_i - cs_i
                    up_row, dn_row = mid + 16 * wide, mid - 16 * wide - 8
                    offset = (16.0 * wide + 8.0) - fine_row
                up_r, up_i = even_r - odd_i, even_i + odd_r
                dn_r, dn_i = even_r + odd_i, even_i - odd_r
                up_rows, dn_rows = slice(up_row, up_row + 8), slice(dn_row, dn_row + 8)
                up, dn = up_r * up_r + up_i * up_i, dn_r * dn_r + dn_i * dn_i
                g_up, g_dn = grad_s[wave, up_rows, :], grad_s[wave, dn_rows, :]
                if sign == 1:
                    dn, g_dn = flip(dn), flip(g_dn)
                else:
                    up, g_up = flip(up), flip(g_up)
                psf_s[wave, up_rows, :] = up
                psf_s[wave, dn_rows, :] = dn
                dn_r, dn_i, up_r, up_i = g_dn * dn_r, g_dn * dn_i, g_up * up_r, g_up * up_i
                p_r, p_i, m_r, m_i = up_r + dn_r, up_i + dn_i, up_r - dn_r, up_i - dn_i
                lines.append(
                    ((p_r, m_i), (p_i, -m_r), (offset * m_r, offset * p_i), (offset * m_i, -(offset * p_r)))
                )
            for kind in range(4):
                (cos_p, sin_p), (cos_m, sin_m) = lines[0][kind], lines[1][kind]
                for block, value in enumerate((cos_p + cos_m, cos_m - cos_p, sin_p + sin_m, sin_p - sin_m)):
                    cot_t[kind, 8 * (wides * block + wide) : 8 * (wides * block + wide) + 8, :] = value
        flat = [cot_t[kind].T for kind in range(4)]
        for group in range(clen // 8):
            rows = slice(8 * group, 8 * group + 8)
            for pair in range(2):
                both = jnp.concatenate([flat[2 * pair][rows], flat[2 * pair + 1][rows]], axis=0)
                cot[wave][32 * group + 16 * pair : 32 * group + 16 * pair + 16, :] = both.astype(jnp.bfloat16)
    psf_store = pltpu.make_async_copy(psf_s, psf_ref, psf_sem)
    psf_store.start()

    sub = lax.broadcasted_iota(jnp.int32, (8, 512), 0).astype(jnp.float32)
    y_sub = sub + (y_low + clen)

    @pl.loop(0, shards)
    def _(shard):
        jobs = [(piece, wave) for piece in range(local // 512) for wave in range(3)]

        def dot(piece, wave):
            return jnp.dot(cot[wave][...], row_tab[wave][shard, :, piece * 512 : (piece + 1) * 512], preferred_element_type=jnp.float32)

        ready = [dot(*job) for job in jobs[:1]]
        for number, (piece, wave) in enumerate(jobs):
            span = slice(piece * 512, (piece + 1) * 512)
            if wave == 0:
                total = [jnp.zeros((8, 512), jnp.float32) for _ in range(4)]
            scale = 2.0 * wave_scales[wave]
            if number + 1 < len(jobs):
                ready.append(dot(*jobs[number + 1]))
            back = ready[number]
            ready[number] = None
            im_sum = up_sum = re_sum = x_sum = jnp.zeros((8, 512), jnp.float32)
            for group in range(clen // 8):
                e_r, e_i, f_r, f_i = [back[32 * group + 8 * n : 32 * group + 8 * n + 8] for n in range(4)]
                b_r = col_tab[wave][shard, 8 * group : 8 * group + 8, span]
                b_i = col_tab[wave][shard, clen + 8 * group : clen + 8 * group + 8, span]
                im_sum = im_sum + (b_r * e_i - b_i * e_r)
                re_sum = re_sum + (b_r * e_r + b_i * e_i)
                x_sum = x_sum + (b_r * f_i - b_i * f_r)
                up_sum = up_sum + im_sum
            total[0] = total[0] + scale * im_sum
            total[1] = total[1] + (scale * two_pi) * (x_mid * im_sum + x_sum)
            total[2] = total[2] + (scale * two_pi) * (y_sub * im_sum - 8.0 * up_sum)
            total[3] = total[3] + 2.0 * re_sum
            if wave == 2:
                rows = [jnp.sum(value, axis=0, keepdims=True) for value in total]
                sums[shard, :, span] = jnp.concatenate(rows, axis=0)

    for slot in range(shards):
        sum_refs[slot][...] = sums[slot]
    psf_store.wait()


def split_pairs(shards):
    if shards == 8:
        return ((3, 7), (4, 5), (1, 6)), 2
    pairs = (shards - 2) // 2
    return tuple((1 + n, 1 + pairs + n) for n in range(pairs)), shards - 1


def on_device(positions, directions, path, amplitude, psf_grad):
    x, y, dir_l, dir_m = positions[0], positions[1], directions[0], directions[1]
    local = path.shape[0]
    tiles = local // LANES
    shards = lax.axis_size("ray")
    rows = lax.axis_size("pix")
    plen = NPIX // rows
    clen = NPIX // shards
    wides = plen // 32
    wide_clen = max(clen, LANES)
    norm = 1.0 / math.sqrt(local * shards)
    pairs, last = split_pairs(shards)
    count = len(pairs)

    def swap(value, ray_even, ray_odd, pix=0):
        moves = []
        for r in range(shards):
            for p in range(rows):
                moves.append((r * rows + p, (r ^ (ray_odd if p % 2 else ray_even)) * rows + (p ^ pix)))
        return lax.ppermute(value, ("ray", "pix"), moves)

    fixed = path * (1.0 / two_pi) - (dir_l * x + dir_m * y)
    packed = jnp.stack([fixed, dir_l, dir_m, amplitude]).reshape(4, tiles, LANES).transpose(1, 0, 2)
    near = [swap(packed, even, odd) for even, odd in pairs]
    extra = swap(packed, last, last)
    far = [swap(part, 0, 0, 1) for part in near]

    weight = jnp.pad(psf_grad, ((0, 0), (0, 0), (0, wide_clen - clen))) if wide_clen > clen else psf_grad
    sizes = (shards, local, plen, clen, wides, norm)
    f32, bf16 = jnp.float32, jnp.bfloat16
    vmem = pl.BlockSpec(memory_space=pltpu.VMEM)
    anywhere = pl.BlockSpec(memory_space=pltpu.HBM)
    psf, *parts = pl.pallas_call(
        functools.partial(psf_kernel, sizes),
        out_shape=[jax.ShapeDtypeStruct((3, plen, wide_clen), f32)] + [jax.ShapeDtypeStruct((4, local), f32)] * shards,
        in_specs=[anywhere] * (shards + 1),
        out_specs=[anywhere] + [vmem] * shards,
        scratch_shapes=[
            pltpu.VMEM((shards, tiles, 4, LANES), f32),
            pltpu.VMEM((4, tiles, shards, LANES), f32),
            pltpu.VMEM((3, 2, tiles, 8 * shards, LANES), f32),
            pltpu.VMEM((3, 2, tiles, 8 * shards + 8, LANES), f32),
            pltpu.VMEM((3, 2, tiles, 8 * shards, LANES), f32),
            pltpu.VMEM((3, 3, tiles, shards + 8, LANES), f32),
            pltpu.VMEM((3, plen, wide_clen), f32),
            pltpu.VMEM((3, plen, wide_clen), f32),
            pltpu.VMEM((4, 32 * wides, wide_clen), f32),
            pltpu.VMEM((shards, 4, local), f32),
            pltpu.SemaphoreType.DMA((shards,)),
            pltpu.SemaphoreType.DMA,
            pltpu.SemaphoreType.DMA,
            *[pltpu.VMEM((shards, 32 * wides, local), bf16)] * 3,
            *[pltpu.VMEM((shards, 2 * clen, local), f32)] * 3,
            *[pltpu.VMEM((2 * wide_clen, local), bf16)] * 3,
            *[pltpu.VMEM((32 * wides, 2 * wide_clen), f32)] * 3,
            *[pltpu.VMEM((4 * clen, 32 * wides), bf16)] * 3,
        ],
        compiler_params=pltpu.CompilerParams(vmem_limit_bytes=62 * 1024 * 1024),
    )(packed, *near, *far, extra, weight)

    psf = psf[..., :clen]

    own_sum, near_sum, far_sum, extra_sum = parts[0], parts[1 : 1 + count], parts[1 + count : 1 + 2 * count], parts[-1]
    near_sum = [near + swap(far, 0, 0, 1) for near, far in zip(near_sum, far_sum)]
    total = own_sum + swap(extra_sum, last, last)
    for part, (even, odd) in zip(near_sum, pairs):
        total = total + swap(part, even, odd)
    bit = rows // 2
    while bit:
        total = total + swap(total, 0, 0, bit)
        bit //= 2
    s1, s2, s3, s4 = total
    grads = jnp.stack(
        [
            s1,
            -two_pi * dir_l * s1,
            -two_pi * dir_m * s1,
            (s2 - two_pi * x * s1) / NPIX,
            (s3 - two_pi * y * s1) / NPIX,
            s4 / amplitude,
        ]
    )
    return (psf, grads)


def solution(mesh):
    in_specs = (P(None, "ray"), P(None, "ray"), P("ray"), P("ray"), P(None, "pix", "ray"))
    out_specs = (P(None, "pix", "ray"), P(None, "ray"))
    return jax.shard_map(on_device, mesh=mesh, in_specs=in_specs, out_specs=out_specs, check_vma=False)
```
